32 devices in a mesh: seq: 16 (over z, y, x), geo: 2 (over core).
Axes of the slice: x: 2, y: 2, z: 4, core: 2. Of those that a mesh axis runs over, the one named last changes fastest.
Arguments:
- cells: bfloat16 [8192, 1024], P(('geo', 'seq')), parts along dimension 0, may hold values from -8 to 8
- anchor_index: int32 [256], P(('geo', 'seq')), parts along dimension 0, may hold values from 0 to 4095, as said below
- queries: bfloat16 [8192, 1024], P(('geo', 'seq')), parts along dimension 0, may hold values from -8 to 8
- norm_gain: float32 [1024], replicated, may hold values from 0.25 to 1.75
- w_qkv: bfloat16 [1024, 3072], P('seq'), may hold values from -1 to 1
- w_out: bfloat16 [1024, 1024], P('seq'), may hold values from -0.1875 to 0.1875
Outputs:
- anchor_out: bfloat16 [256, 1024], P(('geo', 'seq')), parts along dimension 0
- query_out: bfloat16 [8192, 1024], P(('geo', 'seq')), parts along dimension 0
The draws below stay inside these ranges and needn't reach their ends.
There are 2 independent parts, one for each index of `geo`. The reference program is written for one: setup_inputs(seed, part) draws one part's arguments, and reference() takes and returns one part's arrays. A program takes and returns all parts, laid end to end along the dimension named above; an argument that names none is the same for every part. Nothing has to cross between parts.
Inputs may be any that keep to these rules, and one draw needn't show every extreme that they name: `anchor_index`: the 8 anchors of each seq block name cells of the same block of 256 cells; repeats may occur.
All inputs are finite; a program needn't handle non-finite values.
Results may differ from the reference program's by a relative error of at most 0.0091.
Values may be sent and summed in bfloat16 or wider, within the bound.
A program may use at most 64 MiB of HBM per device.

```python
import jax
import jax.numpy as jnp
from jax import lax

D = 1024
HEADS = 16
HEAD_DIM = 64
C_DEV = 256
A_DEV = 8
CELLS = 4096
ANCHORS = 128
QUERIES = 4096


def drawn_rows(key, rows, width):
    return jnp.clip(jax.random.normal(key, (rows, width), jnp.float32), -6.0, 6.0)


def draw_cells(key, part):
    key = jax.random.fold_in(key, 11)
    values = drawn_rows(key, CELLS, D)
    return values.astype(jnp.bfloat16)


def draw_queries(key, part):
    key = jax.random.fold_in(key, 12)
    values = drawn_rows(key, QUERIES, D)
    return values.astype(jnp.bfloat16)


def draw_w_qkv(key, part):
    key = jax.random.fold_in(key, 13)
    values = jnp.clip(jax.random.normal(key, (D, 3 * D), jnp.float32), -6.0, 6.0) * D ** (-0.5)
    return values.astype(jnp.bfloat16)


def draw_anchor_index(key, part):
    key = jax.random.fold_in(key, 7)
    position = jnp.arange(ANCHORS, dtype=jnp.int32)
    block = position // A_DEV
    offset = jax.random.randint(key, (ANCHORS,), 0, C_DEV, dtype=jnp.int32)
    offset = jnp.where(position == 0, 0, offset)
    offset = jnp.where(position == ANCHORS - 1, C_DEV - 1, offset)
    return (block * C_DEV + offset).astype(jnp.int32)


def block_scale(key, extent, shards, least, largest):
    def one(dim, blocks):
        heights = jax.random.uniform(jax.random.fold_in(jax.random.fold_in(key, 6), dim), (blocks,), jnp.float32, least / len(shards), largest / len(shards))
        return jnp.repeat(jnp.exp(heights), extent[dim] // blocks).reshape((-1,) + (1,) * (len(extent) - dim - 1))

    factor_of = one(*shards[0])
    for cut in shards[1:]:
        factor_of = factor_of * one(*cut)
    return factor_of


def normal_values(rng, shape, spread, most, pieces=(), held_as=jnp.bfloat16):
    array = jax.random.normal(rng, shape, jnp.float32) * spread
    if len(pieces) > 0:
        array = block_scale(rng, shape, pieces, -0.22, 0.18) * array
    return jnp.clip(array, min=-most, max=most).astype(held_as)


def setup_inputs(seed: int = 0, part: int = 0) -> dict:
    keys = jax.random.split(jax.random.key(seed), 7)
    part_splits = jax.random.split(jax.random.fold_in(keys[6], part), 7)
    return {
        "cells": draw_cells(jax.random.fold_in(jax.random.fold_in(keys[6], part), 71), part),
        "anchor_index": draw_anchor_index(jax.random.fold_in(jax.random.fold_in(keys[6], part), 71), part),
        "queries": draw_queries(jax.random.fold_in(jax.random.fold_in(keys[6], part), 71), part),
        "norm_gain": jnp.clip(1.0 + 0.15 * jax.random.normal(keys[3], (D,), jnp.float32), 0.25, 1.75),
        "w_qkv": draw_w_qkv(jax.random.fold_in(keys[6], 71), part),
        "w_out": normal_values(keys[5], (D, D), D ** -0.5, 0.1875, ((0, 16),)),
    }


def normalize(rows, norm_gain):
    values = rows.astype(jnp.float32)
    scale = lax.rsqrt(lax.optimization_barrier(jnp.mean(values * values, axis=-1, keepdims=True)) + 1e-05)
    return (values * scale * norm_gain).astype(jnp.bfloat16)

def attend(query_rows, key_rows, value_rows):
    count = query_rows.shape[0]
    factor = HEAD_DIM ** (-0.5)
    qh = query_rows.reshape(count, HEADS, HEAD_DIM).transpose(1, 0, 2)
    kh = key_rows.reshape(key_rows.shape[0], HEADS, HEAD_DIM).transpose(1, 0, 2)
    vh = value_rows.reshape(value_rows.shape[0], HEADS, HEAD_DIM).transpose(1, 0, 2)

    def single(items):
        qpart, kpart, vpart = items
        scores = jnp.dot(qpart, kpart.T, preferred_element_type=jnp.float32) * factor
        peak = lax.optimization_barrier(jnp.max(scores, axis=-1, keepdims=True))
        expo = jnp.exp(scores - peak)
        total = lax.optimization_barrier(jnp.sum(expo, axis=-1, keepdims=True))
        mixed = jnp.dot(expo.astype(jnp.bfloat16), vpart, preferred_element_type=jnp.float32)
        return (mixed / total).astype(jnp.bfloat16)
    result = lax.map(single, (qh, kh, vh))
    return result.transpose(1, 0, 2).reshape(count, D)

def reference(cells, anchor_index, queries, norm_gain, w_qkv, w_out):
    anchors = jnp.take(cells, anchor_index, axis=0)
    norm_a = normalize(anchors, norm_gain)
    norm_q = normalize(queries, norm_gain)
    qkv_a = jnp.dot(norm_a, w_qkv, preferred_element_type=jnp.float32).astype(jnp.bfloat16)
    q_a = qkv_a[:, :D]
    k_a = qkv_a[:, D:2 * D]
    v_a = qkv_a[:, 2 * D:]
    q_q = jnp.dot(norm_q, w_qkv[:, :D], preferred_element_type=jnp.float32).astype(jnp.bfloat16)
    ctx_a = attend(q_a, k_a, v_a)
    ctx_q = attend(q_q, k_a, v_a)
    anchor_out = jnp.dot(ctx_a, w_out, preferred_element_type=jnp.float32).astype(jnp.bfloat16)
    query_out = jnp.dot(ctx_q, w_out, preferred_element_type=jnp.float32).astype(jnp.bfloat16)
    return (anchor_out, query_out)
```

```python
import functools

import jax
import jax.numpy as jnp
from jax import lax
from jax.experimental import pallas as pl
from jax.experimental.pallas import tpu as pltpu
from jax.sharding import PartitionSpec as P

HEADS = 16
PLANE = 4
LANES = 128
MESH = pl.DeviceIdType.MESH


def normalize(rows, norm_gain):
    values = rows.astype(jnp.float32)
    scale = lax.rsqrt(jnp.mean(values * values, axis=-1, keepdims=True) + 1e-05)
    return (values * scale * norm_gain).astype(jnp.bfloat16)


def split_heads(rows, heads):
    return rows.reshape(rows.shape[0], heads, rows.shape[1] // heads).transpose(1, 0, 2)


def attend_whole(query_rows, key_rows, value_rows, heads):
    count, width = query_rows.shape
    factor = (width // heads) ** (-0.5)

    def single(items):
        qpart, kpart, vpart = items
        scores = jnp.dot(qpart, kpart.T, preferred_element_type=jnp.float32) * factor
        peak = jnp.max(scores, axis=-1, keepdims=True)
        expo = jnp.exp(scores - peak)
        total = jnp.sum(expo, axis=-1, keepdims=True)
        mixed = jnp.dot(expo.astype(jnp.bfloat16), vpart, preferred_element_type=jnp.float32)
        return (mixed / total).astype(jnp.bfloat16)

    result = lax.map(
        single,
        (
            split_heads(query_rows, heads),
            split_heads(key_rows, heads),
            split_heads(value_rows, heads),
        ),
    )
    return result.transpose(1, 0, 2).reshape(count, width)


def gathered(cells, anchor_index, queries, norm_gain, w_qkv, w_out):
    heads = HEADS
    width = cells.shape[1]
    anchor_rows = anchor_index.shape[0]
    local_index = anchor_index - lax.axis_index("seq") * cells.shape[0]
    anchors = jnp.take(cells, local_index, axis=0)
    norm_a = normalize(anchors, norm_gain)
    norm_q = normalize(queries, norm_gain)
    piece = lax.all_gather(w_qkv, "seq", axis=0, tiled=True)
    total_a = jnp.dot(norm_a, piece, preferred_element_type=jnp.float32)
    total_q = jnp.dot(norm_q, piece[:, :width], preferred_element_type=jnp.float32)
    qkv_a = total_a.astype(jnp.bfloat16)
    q_q = total_q.astype(jnp.bfloat16)
    all_query = jnp.concatenate([qkv_a[:, :width], q_q], axis=0)
    keys_values = lax.all_gather(qkv_a[:, width:], "seq", axis=0, tiled=True)
    context = attend_whole(all_query, keys_values[:, :width], keys_values[:, width:], heads)
    projected = jnp.dot(
        context,
        lax.all_gather(w_out, "seq", axis=0, tiled=True),
        preferred_element_type=jnp.float32,
    )
    projected = projected.astype(jnp.bfloat16)
    return (projected[:anchor_rows], projected[anchor_rows:])


def kernel(
    lines,
    index_ref,
    cells_ref,
    queries_ref,
    gain_ref,
    w_qkv_ref,
    w_out_ref,
    anchor_out_ref,
    query_out_ref,
    norm_ref,
    q_ref,
    ctx_ref,
    na_all,
    wkv,
    kv_all,
    wq_all,
    wo_all,
    send_sem,
    na_sem,
    a2a_sem,
    kv_sem,
    wq_sem,
    wo_sem,
    wq_sib_sem,
    wo_sib_sem,
):
    count = lines * PLANE
    me = lax.axis_index("seq")
    core = lax.axis_index("geo")
    line = me // PLANE
    spot = me % PLANE
    width = cells_ref.shape[1]
    half = width // 2
    mine = pl.ds(pl.multiple_of(core * half, LANES), half)
    other = pl.ds(pl.multiple_of((1 - core) * half, LANES), half)
    anchors = index_ref.shape[0]
    rows = queries_ref.shape[0]

    barrier = pltpu.get_barrier_semaphore()
    for k in range(1, count):
        pl.semaphore_signal(
            barrier, inc=1, device_id={"seq": (me + k) % count}, device_id_type=MESH
        )
    pl.semaphore_signal(barrier, inc=1, device_id={"geo": 1 - core}, device_id_type=MESH)

    started = []

    def send(src, dst, sem, target):
        copy = pltpu.make_async_remote_copy(
            src_ref=src,
            dst_ref=dst,
            send_sem=send_sem.at[len(started)],
            recv_sem=sem,
            device_id=target,
            device_id_type=MESH,
        )
        copy.start()
        started.append(copy)

    def arrived(dst, sem):
        pltpu.make_async_remote_copy(
            src_ref=dst,
            dst_ref=dst,
            send_sem=send_sem.at[0],
            recv_sem=sem,
            device_id={"geo": 1 - core},
            device_id_type=MESH,
        ).wait_recv()

    gain = gain_ref[...]

    row = lax.broadcasted_iota(jnp.int32, (anchors, cells_ref.shape[0]), 0)
    column = lax.broadcasted_iota(jnp.int32, (anchors, cells_ref.shape[0]), 1)
    wanted = jnp.zeros_like(row)
    for a in range(anchors):
        wanted = jnp.where(row == a, index_ref[a] - me * cells_ref.shape[0], wanted)
    pick = jnp.where(wanted == column, 1.0, 0.0).astype(jnp.bfloat16)
    picked = jnp.dot(pick, cells_ref[...], preferred_element_type=jnp.float32)
    scale = lax.rsqrt(jnp.mean(picked * picked, axis=-1, keepdims=True) + 1e-05)
    norm_a = picked * scale * gain
    na_all[line, spot] = jnp.concatenate([norm_a[:, :half], norm_a[:, half:]], axis=0).astype(
        jnp.bfloat16
    )
    norm_ref[pl.ds(rows, 2 * anchors), :] = jnp.concatenate([norm_a, norm_a], axis=0).astype(
        jnp.bfloat16
    )
    wq_all[line, spot] = w_qkv_ref[:, :width]
    wo_all[line, spot] = w_out_ref[...]
    wkv[me] = w_qkv_ref[:, pl.ds(pl.multiple_of(width + me * LANES, LANES), LANES)]

    pl.semaphore_wait(barrier, count)

    def on_line(k):
        return (line + k) % lines

    def on_plane(k):
        return (spot + k) % PLANE

    def line_target(k):
        return {"seq": on_line(k) * PLANE + spot}

    def plane_target(k):
        return {"seq": line * PLANE + on_plane(k)}

    sibling = {"geo": 1 - core}

    for k in range(1, lines):
        block = na_all.at[line, spot]
        send(block, block, na_sem.at[line], line_target(k))
    for k in range(1, count):
        to = (me + k) % count
        start = pl.multiple_of(width + to * LANES, LANES)
        send(w_qkv_ref.at[:, pl.ds(start, LANES)], wkv.at[me], a2a_sem.at[me], {"seq": to})

    def to_line(whole, sem):
        block = whole.at[line, spot, :, mine]
        for k in range(1, lines):
            send(block, block, sem.at[line, spot], line_target(k))

    def to_plane(whole, sem, at):
        block = whole.at[at, spot, :, mine]
        for k in range(1, PLANE):
            send(block, block, sem.at[at, spot], plane_target(k))

    def to_sibling(whole, sem, at, where):
        block = whole.at[at, where, :, mine]
        send(block, block, sem.at[at, where], sibling)

    to_line(wq_all, wq_sem)
    to_plane(wq_all, wq_sem, line)
    to_line(wo_all, wo_sem)

    values = queries_ref[...].astype(jnp.float32)
    scale = lax.rsqrt(jnp.mean(values * values, axis=-1, keepdims=True) + 1e-05)
    norm_ref[pl.ds(0, rows), :] = (values * scale * gain).astype(jnp.bfloat16)

    for k in range(1, lines):
        arrived(na_all.at[on_line(k), spot], na_sem.at[on_line(k)])
    for k in range(1, PLANE):
        block = na_all.at[:, spot]
        send(block, block, na_sem.at[lines + spot], plane_target(k))
    for k in range(1, lines):
        at = on_line(k)
        arrived(wq_all.at[at, spot, :, mine], wq_sem.at[at, spot])
        to_plane(wq_all, wq_sem, at)
        to_sibling(wq_all, wq_sib_sem, at, spot)

    for k in range(1, PLANE):
        arrived(na_all.at[:, on_plane(k)], na_sem.at[lines + on_plane(k)])
    for k in range(1, count):
        source = (me + k) % count
        arrived(wkv.at[source], a2a_sem.at[source])
    packed = na_all[...].reshape(count * 2 * anchors, half)
    slab = wkv[...].reshape(width, LANES)
    low = jnp.dot(packed, slab[:half], preferred_element_type=jnp.float32)
    high = jnp.dot(packed, slab[half:], preferred_element_type=jnp.float32)
    low = low.reshape(count, 2 * anchors, LANES)[:, :anchors]
    high = high.reshape(count, 2 * anchors, LANES)[:, anchors:]
    kv_all[line, spot] = (low + high).reshape(count * anchors, LANES).astype(jnp.bfloat16)

    for k in range(1, lines):
        block = kv_all.at[line, spot]
        send(block, block, kv_sem.at[line], line_target(k))
    to_plane(wo_all, wo_sem, line)
    for k in range(1, lines):
        arrived(kv_all.at[on_line(k), spot], kv_sem.at[on_line(k)])
    for k in range(1, PLANE):
        block = kv_all.at[:, spot]
        send(block, block, kv_sem.at[lines + spot], plane_target(k))
    for k in range(1, lines):
        at = on_line(k)
        arrived(wo_all.at[at, spot, :, mine], wo_sem.at[at, spot])
        to_plane(wo_all, wo_sem, at)
        to_sibling(wo_all, wo_sib_sem, at, spot)

    def rest_to_sibling(whole, sem, sib_sem):
        for j in range(lines):
            for k in range(1, PLANE):
                at, where = on_line(j), on_plane(k)
                arrived(whole.at[at, where, :, mine], sem.at[at, where])
                to_sibling(whole, sib_sem, at, where)

    def from_sibling(whole, sib_sem):
        for j in range(lines):
            for k in range(PLANE):
                if j or k:
                    at, where = on_line(j), on_plane(k)
                    arrived(whole.at[at, where, :, other], sib_sem.at[at, where])

    rest_to_sibling(wq_all, wq_sem, wq_sib_sem)
    from_sibling(wq_all, wq_sib_sem)
    step = 2 * LANES
    for j in range(width // step):
        columns = pl.ds(j * step, step)
        block = wq_all[:, :, :, columns].reshape(width, step)
        q_ref[:, columns] = jnp.dot(
            norm_ref[...], block, preferred_element_type=jnp.float32
        ).astype(jnp.bfloat16)

    for k in range(1, PLANE):
        arrived(kv_all.at[:, on_plane(k)], kv_sem.at[lines + on_plane(k)])

    head = width // HEADS
    factor = head ** (-0.5)
    keys = count * anchors
    upper = lax.broadcasted_iota(jnp.int32, (keys, LANES), 1) >= head
    upper_ctx = lax.broadcasted_iota(jnp.int32, (norm_ref.shape[0], LANES), 1) >= head

    def blocks(pair):
        block = kv_all[pair // PLANE, pair % PLANE]
        zero = jnp.zeros_like(block)
        return jnp.concatenate([jnp.where(upper, zero, block), jnp.where(upper, block, zero)], axis=0)

    pairs = HEADS // 2
    for pair in range(pairs):
        columns = pl.ds(pair * LANES, LANES)
        scores = lax.dot_general(
            q_ref[:, columns],
            blocks(pair),
            (((1,), (1,)), ((), ())),
            preferred_element_type=jnp.float32,
        )
        scores = scores * factor
        expos, totals = [], []
        for side in range(2):
            part = scores[:, side * keys : (side + 1) * keys]
            expo = jnp.exp(part - jnp.max(part, axis=-1, keepdims=True))
            totals.append(jnp.sum(expo, axis=-1, keepdims=True))
            expos.append(expo.astype(jnp.bfloat16))
        mixed = jnp.dot(
            jnp.concatenate(expos, axis=1), blocks(pairs + pair), preferred_element_type=jnp.float32
        )
        total = jnp.where(upper_ctx, totals[1], totals[0])
        ctx_ref[:, columns] = (mixed / total).astype(jnp.bfloat16)

    rest_to_sibling(wo_all, wo_sem, wo_sib_sem)
    from_sibling(wo_all, wo_sib_sem)
    for j in range(width // step):
        columns = pl.ds(j * step, step)
        block = wo_all[:, :, :, columns].reshape(width, step)
        result = jnp.dot(ctx_ref[...], block, preferred_element_type=jnp.float32)
        query_out_ref[:, columns] = result[:rows].astype(jnp.bfloat16)
        anchor_out_ref[:, columns] = result[rows : rows + anchors].astype(jnp.bfloat16)

    for copy in started:
        copy.wait_send()


def fused(lines, cells, anchor_index, queries, norm_gain, w_qkv, w_out):
    rows, width = queries.shape
    anchors = anchor_index.shape[0]
    depth = w_out.shape[0]
    count = lines * PLANE
    padded = rows + 2 * anchors
    vmem = pl.BlockSpec(memory_space=pltpu.VMEM)
    grid = (lines, PLANE)
    bf16 = jnp.bfloat16
    copies = 2 * (lines - 1 + PLANE - 1) + count - 1
    copies += 2 * (lines - 1 + lines * (PLANE - 1) + count - 1)
    return pl.pallas_call(
        functools.partial(kernel, lines),
        out_shape=(
            jax.ShapeDtypeStruct((anchors, width), bf16),
            jax.ShapeDtypeStruct((rows, width), bf16),
        ),
        in_specs=[pl.BlockSpec(memory_space=pltpu.SMEM)] + [vmem] * 5,
        out_specs=(vmem, vmem),
        scratch_shapes=[
            pltpu.VMEM((padded, width), bf16),
            pltpu.VMEM((padded, width), bf16),
            pltpu.VMEM((padded, width), bf16),
            pltpu.VMEM((*grid, 2 * anchors, width // 2), bf16),
            pltpu.VMEM((count, depth, LANES), bf16),
            pltpu.VMEM((*grid, count * anchors, LANES), bf16),
            pltpu.VMEM((*grid, depth, width), bf16),
            pltpu.VMEM((*grid, depth, width), bf16),
            pltpu.SemaphoreType.DMA((copies,)),
            pltpu.SemaphoreType.DMA((lines + PLANE,)),
            pltpu.SemaphoreType.DMA((count,)),
            pltpu.SemaphoreType.DMA((lines + PLANE,)),
            pltpu.SemaphoreType.DMA(grid),
            pltpu.SemaphoreType.DMA(grid),
            pltpu.SemaphoreType.DMA(grid),
            pltpu.SemaphoreType.DMA(grid),
        ],
        compiler_params=pltpu.CompilerParams(
            collective_id=0, has_side_effects=True, vmem_limit_bytes=40 * 1024 * 1024
        ),
        cost_estimate=pl.CostEstimate(
            flops=4 * padded * width * width, bytes_accessed=4 * width * width, transcendentals=0
        ),
    )(anchor_index, cells, queries, norm_gain.reshape(1, -1), w_qkv, w_out)


def solution(mesh):
    count, parts = mesh.shape["seq"], mesh.shape["geo"]

    def local(cells, anchor_index, queries, norm_gain, w_qkv, w_out):
        width = cells.shape[1]
        args = (cells, anchor_index, queries, norm_gain, w_qkv, w_out)
        tiles = (
            parts == 2
            and count % PLANE == 0
            and count * LANES == 2 * width
            and HEADS * LANES == 2 * width
            and count * anchor_index.shape[0] == LANES
        )
        if tiles:
            return fused(count // PLANE, *args)
        return gathered(*args)

    placed = (
        P(("geo", "seq"), None),
        P(("geo", "seq")),
        P(("geo", "seq"), None),
        P(),
        P("seq", None),
        P("seq", None),
    )
    return jax.shard_map(
        local,
        mesh=mesh,
        in_specs=placed,
        out_specs=(P(("geo", "seq"), None), P(("geo", "seq"), None)),
        check_vma=False,
    )
```

```python
import functools

import jax
import jax.numpy as jnp
from jax import lax
from jax.experimental import pallas as pl
from jax.experimental.pallas import tpu as pltpu
from jax.sharding import PartitionSpec as P

HEADS = 16
PLANE = 4
LANES = 128
MESH = pl.DeviceIdType.MESH


def normalize(rows, norm_gain):
    values = rows.astype(jnp.float32)
    scale = lax.rsqrt(jnp.mean(values * values, axis=-1, keepdims=True) + 1e-05)
    return (values * scale * norm_gain).astype(jnp.bfloat16)


def split_heads(rows, heads):
    return rows.reshape(rows.shape[0], heads, rows.shape[1] // heads).transpose(1, 0, 2)


def attend_whole(query_rows, key_rows, value_rows, heads):
    count, width = query_rows.shape
    factor = (width // heads) ** (-0.5)

    def single(items):
        qpart, kpart, vpart = items
        scores = jnp.dot(qpart, kpart.T, preferred_element_type=jnp.float32) * factor
        peak = jnp.max(scores, axis=-1, keepdims=True)
        expo = jnp.exp(scores - peak)
        total = jnp.sum(expo, axis=-1, keepdims=True)
        mixed = jnp.dot(expo.astype(jnp.bfloat16), vpart, preferred_element_type=jnp.float32)
        return (mixed / total).astype(jnp.bfloat16)

    result = lax.map(
        single,
        (
            split_heads(query_rows, heads),
            split_heads(key_rows, heads),
            split_heads(value_rows, heads),
        ),
    )
    return result.transpose(1, 0, 2).reshape(count, width)


def gathered(cells, anchor_index, queries, norm_gain, w_qkv, w_out):
    heads = HEADS
    width = cells.shape[1]
    anchor_rows = anchor_index.shape[0]
    local_index = anchor_index - lax.axis_index("seq") * cells.shape[0]
    anchors = jnp.take(cells, local_index, axis=0)
    norm_a = normalize(anchors, norm_gain)
    norm_q = normalize(queries, norm_gain)
    piece = lax.all_gather(w_qkv, "seq", axis=0, tiled=True)
    total_a = jnp.dot(norm_a, piece, preferred_element_type=jnp.float32)
    total_q = jnp.dot(norm_q, piece[:, :width], preferred_element_type=jnp.float32)
    qkv_a = total_a.astype(jnp.bfloat16)
    q_q = total_q.astype(jnp.bfloat16)
    all_query = jnp.concatenate([qkv_a[:, :width], q_q], axis=0)
    keys_values = lax.all_gather(qkv_a[:, width:], "seq", axis=0, tiled=True)
    context = attend_whole(all_query, keys_values[:, :width], keys_values[:, width:], heads)
    projected = jnp.dot(
        context,
        lax.all_gather(w_out, "seq", axis=0, tiled=True),
        preferred_element_type=jnp.float32,
    )
    projected = projected.astype(jnp.bfloat16)
    return (projected[:anchor_rows], projected[anchor_rows:])


def kernel(
    lines,
    index_ref,
    cells_hbm,
    queries_hbm,
    gain_hbm,
    w_qkv_ref,
    w_out_ref,
    anchor_out_ref,
    query_out_ref,
    cells_ref,
    queries_ref,
    gain_ref,
    norm_ref,
    q_ref,
    ctx_ref,
    na_all,
    wkv,
    kv_all,
    wq_all,
    wo_all,
    load_sem,
    send_sem,
    na_sem,
    a2a_sem,
    kv_sem,
    wq_sem,
    wo_sem,
    wq_sib_sem,
    wo_sib_sem,
):
    count = lines * PLANE
    me = lax.axis_index("seq")
    core = lax.axis_index("geo")
    line = me // PLANE
    spot = me % PLANE
    width = cells_ref.shape[1]
    half = width // 2
    mine = pl.ds(pl.multiple_of(core * half, LANES), half)
    other = pl.ds(pl.multiple_of((1 - core) * half, LANES), half)
    anchors = index_ref.shape[0]
    rows = queries_ref.shape[0]

    flip_x = 1 - 2 * (spot % 2)
    flip_y = 2 - 4 * (spot // 2)
    near = spot + flip_x * (1 - core) + flip_y * core
    far = spot + flip_y * (1 - core) + flip_x * core
    cross = spot + flip_x + flip_y

    barrier = pltpu.get_barrier_semaphore()
    for k in range(1, count):
        pl.semaphore_signal(
            barrier, inc=1, device_id={"seq": (me + k) % count}, device_id_type=MESH
        )
    pl.semaphore_signal(barrier, inc=1, device_id={"geo": 1 - core}, device_id_type=MESH)

    start = pl.multiple_of(width + me * LANES, LANES)
    loads = []
    for source, target in (
        (cells_hbm, cells_ref),
        (gain_hbm, gain_ref),
        (w_qkv_ref.at[:, pl.ds(0, width)], wq_all.at[line, spot]),
        (w_qkv_ref.at[:, pl.ds(start, LANES)], wkv.at[me]),
        (w_out_ref, wo_all.at[line, spot]),
        (queries_hbm, queries_ref),
    ):
        load = pltpu.make_async_copy(source, target, load_sem.at[len(loads)])
        load.start()
        loads.append(load)

    started = []

    def send(src, dst, sem, target):
        copy = pltpu.make_async_remote_copy(
            src_ref=src,
            dst_ref=dst,
            send_sem=send_sem.at[len(started)],
            recv_sem=sem,
            device_id=target,
            device_id_type=MESH,
        )
        copy.start()
        started.append(copy)

    def arrived(dst, sem):
        pltpu.make_async_remote_copy(
            src_ref=dst,
            dst_ref=dst,
            send_sem=send_sem.at[0],
            recv_sem=sem,
            device_id={"geo": 1 - core},
            device_id_type=MESH,
        ).wait_recv()

    loads[0].wait()
    loads[1].wait()
    gain = gain_ref[...]

    row = lax.broadcasted_iota(jnp.int32, (anchors, cells_ref.shape[0]), 0)
    column = lax.broadcasted_iota(jnp.int32, (anchors, cells_ref.shape[0]), 1)
    wanted = jnp.zeros_like(row)
    for a in range(anchors):
        wanted = jnp.where(row == a, index_ref[a] - me * cells_ref.shape[0], wanted)
    pick = jnp.where(wanted == column, 1.0, 0.0).astype(jnp.bfloat16)
    picked = jnp.dot(pick, cells_ref[...], preferred_element_type=jnp.float32)
    scale = lax.rsqrt(jnp.mean(picked * picked, axis=-1, keepdims=True) + 1e-05)
    norm_a = picked * scale * gain
    na_all[line, spot] = jnp.concatenate([norm_a[:, :half], norm_a[:, half:]], axis=0).astype(
        jnp.bfloat16
    )
    norm_ref[pl.ds(rows, 2 * anchors), :] = jnp.concatenate([norm_a, norm_a], axis=0).astype(
        jnp.bfloat16
    )
    for load in loads[2:5]:
        load.wait()

    pl.semaphore_wait(barrier, count)

    def on_line(k):
        return (line + k) % lines

    def on_plane(k):
        return (spot + k) % PLANE

    def line_target(k):
        return {"seq": on_line(k) * PLANE + spot}

    def plane_target(where):
        return {"seq": line * PLANE + where}

    sibling = {"geo": 1 - core}

    def to_line(whole, sem):
        block = whole.at[line, spot, :, mine]
        for k in range(1, lines):
            send(block, block, sem.at[line, spot], line_target(k))

    def to_plane(whole, sem, at):
        block = whole.at[at, spot, :, mine]
        send(block, block, sem.at[at, spot], plane_target(near))
        send(block, block, sem.at[at, spot], plane_target(far))

    def to_cross(whole, sem, at):
        block = whole.at[at, near, :, mine]
        send(block, block, sem.at[at, near], plane_target(far))

    def to_sibling(whole, sem, at, where):
        block = whole.at[at, where, :, mine]
        send(block, block, sem.at[at, where], sibling)

    def weight_arrived(whole, sem, at, where):
        arrived(whole.at[at, where, :, mine], sem.at[at, where])

    for k in range(1, lines):
        block = na_all.at[line, spot]
        send(block, block, na_sem.at[line], line_target(k))
    for k in range(1, count):
        to = (me + k) % count
        start = pl.multiple_of(width + to * LANES, LANES)
        send(w_qkv_ref.at[:, pl.ds(start, LANES)], wkv.at[me], a2a_sem.at[me], {"seq": to})
    to_line(wq_all, wq_sem)
    to_plane(wq_all, wq_sem, line)

    for k in range(1, lines):
        arrived(na_all.at[on_line(k), spot], na_sem.at[on_line(k)])
    for k in range(1, PLANE):
        block = na_all.at[:, spot]
        send(block, block, na_sem.at[lines + spot], plane_target(on_plane(k)))

    loads[5].wait()
    values = queries_ref[...].astype(jnp.float32)
    scale = lax.rsqrt(jnp.mean(values * values, axis=-1, keepdims=True) + 1e-05)
    norm_ref[pl.ds(0, rows), :] = (values * scale * gain).astype(jnp.bfloat16)

    for k in range(1, lines):
        at = on_line(k)
        weight_arrived(wq_all, wq_sem, at, spot)
        to_plane(wq_all, wq_sem, at)
        to_sibling(wq_all, wq_sib_sem, at, spot)
    to_line(wo_all, wo_sem)

    for k in range(1, PLANE):
        arrived(na_all.at[:, on_plane(k)], na_sem.at[lines + on_plane(k)])
    for k in range(1, count):
        source = (me + k) % count
        arrived(wkv.at[source], a2a_sem.at[source])
    packed = na_all[...].reshape(count * 2 * anchors, half)
    slab = wkv[...].reshape(width, LANES)
    low = jnp.dot(packed, slab[:half], preferred_element_type=jnp.float32)
    high = jnp.dot(packed, slab[half:], preferred_element_type=jnp.float32)
    low = low.reshape(count, 2 * anchors, LANES)[:, :anchors]
    high = high.reshape(count, 2 * anchors, LANES)[:, anchors:]
    kv_all[line, spot] = (low + high).reshape(count * anchors, LANES).astype(jnp.bfloat16)

    for k in range(1, lines):
        block = kv_all.at[line, spot]
        send(block, block, kv_sem.at[line], line_target(k))
    for k in range(lines):
        weight_arrived(wq_all, wq_sem, on_line(k), near)
        to_cross(wq_all, wq_sem, on_line(k))
        to_sibling(wq_all, wq_sib_sem, on_line(k), near)
    for k in range(1, lines):
        arrived(kv_all.at[on_line(k), spot], kv_sem.at[on_line(k)])
    block = kv_all.at[:, spot]
    send(block, block, kv_sem.at[lines + spot], plane_target(near))
    send(block, block, kv_sem.at[lines + spot], plane_target(far))
    to_plane(wo_all, wo_sem, line)
    for k in range(1, lines):
        at = on_line(k)
        weight_arrived(wo_all, wo_sem, at, spot)
        to_plane(wo_all, wo_sem, at)
        to_sibling(wo_all, wo_sib_sem, at, spot)
    arrived(kv_all.at[:, near], kv_sem.at[lines + near])
    block = kv_all.at[:, near]
    send(block, block, kv_sem.at[lines + near], plane_target(far))

    for where in (far, cross):
        for k in range(lines):
            weight_arrived(wq_all, wq_sem, on_line(k), where)
            to_sibling(wq_all, wq_sib_sem, on_line(k), where)

    def from_sibling(whole, sib_sem):
        for j in range(lines):
            for k in range(PLANE):
                if j or k:
                    at, where = on_line(j), on_plane(k)
                    arrived(whole.at[at, where, :, other], sib_sem.at[at, where])

    from_sibling(wq_all, wq_sib_sem)
    step = 2 * LANES

    later = [(on_line(k), near) for k in range(lines)]
    later += [(on_line(k), far) for k in range(lines)]
    later += [(on_line(k), cross) for k in range(lines)]

    def pass_on(steps):
        for _ in range(steps):
            if later:
                first = len(later) > 2 * lines
                at, where = later.pop(0)
                weight_arrived(wo_all, wo_sem, at, where)
                if first:
                    to_cross(wo_all, wo_sem, at)
                to_sibling(wo_all, wo_sib_sem, at, where)

    for j in range(width // step):
        columns = pl.ds(j * step, step)
        block = wq_all[:, :, :, columns].reshape(width, step)
        q_ref[:, columns] = jnp.dot(
            norm_ref[...], block, preferred_element_type=jnp.float32
        ).astype(jnp.bfloat16)

    arrived(kv_all.at[:, far], kv_sem.at[lines + far])
    arrived(kv_all.at[:, cross], kv_sem.at[lines + cross])

    head = width // HEADS
    factor = head ** (-0.5)
    keys = count * anchors
    upper = lax.broadcasted_iota(jnp.int32, (keys, LANES), 1) >= head
    upper_ctx = lax.broadcasted_iota(jnp.int32, (norm_ref.shape[0], LANES), 1) >= head

    def blocks(pair):
        block = kv_all[pair // PLANE, pair % PLANE]
        zero = jnp.zeros_like(block)
        return jnp.concatenate([jnp.where(upper, zero, block), jnp.where(upper, block, zero)], axis=0)

    pairs = HEADS // 2
    for pair in range(pairs):
        pass_on(2)
        columns = pl.ds(pair * LANES, LANES)
        scores = lax.dot_general(
            q_ref[:, columns],
            blocks(pair),
            (((1,), (1,)), ((), ())),
            preferred_element_type=jnp.float32,
        )
        scores = scores * factor
        expos, totals = [], []
        for side in range(2):
            part = scores[:, side * keys : (side + 1) * keys]
            expo = jnp.exp(part - jnp.max(part, axis=-1, keepdims=True))
            totals.append(jnp.sum(expo, axis=-1, keepdims=True))
            expos.append(expo.astype(jnp.bfloat16))
        mixed = jnp.dot(
            jnp.concatenate(expos, axis=1), blocks(pairs + pair), preferred_element_type=jnp.float32
        )
        total = jnp.where(upper_ctx, totals[1], totals[0])
        ctx_ref[:, columns] = (mixed / total).astype(jnp.bfloat16)

    pass_on(len(later))
    from_sibling(wo_all, wo_sib_sem)
    for j in range(width // step):
        columns = pl.ds(j * step, step)
        block = wo_all[:, :, :, columns].reshape(width, step)
        result = jnp.dot(ctx_ref[...], block, preferred_element_type=jnp.float32)
        query_out_ref[:, columns] = result[:rows].astype(jnp.bfloat16)
        anchor_out_ref[:, columns] = result[rows : rows + anchors].astype(jnp.bfloat16)

    for copy in started:
        copy.wait_send()


def fused(lines, cells, anchor_index, queries, norm_gain, w_qkv, w_out):
    rows, width = queries.shape
    anchors = anchor_index.shape[0]
    depth = w_out.shape[0]
    count = lines * PLANE
    padded = rows + 2 * anchors
    vmem = pl.BlockSpec(memory_space=pltpu.VMEM)
    grid = (lines, PLANE)
    bf16 = jnp.bfloat16
    copies = 2 * (lines - 1 + PLANE - 1) + count - 1
    copies += 2 * (lines - 1 + lines * (PLANE - 1) + count - 1)
    hbm = pl.BlockSpec(memory_space=pltpu.HBM)
    return pl.pallas_call(
        functools.partial(kernel, lines),
        out_shape=(
            jax.ShapeDtypeStruct((anchors, width), bf16),
            jax.ShapeDtypeStruct((rows, width), bf16),
        ),
        in_specs=[pl.BlockSpec(memory_space=pltpu.SMEM)] + [hbm] * 5,
        out_specs=(vmem, vmem),
        scratch_shapes=[
            pltpu.VMEM(cells.shape, bf16),
            pltpu.VMEM(queries.shape, bf16),
            pltpu.VMEM((1, width), jnp.float32),
            pltpu.VMEM((padded, width), bf16),
            pltpu.VMEM((padded, width), bf16),
            pltpu.VMEM((padded, width), bf16),
            pltpu.VMEM((*grid, 2 * anchors, width // 2), bf16),
            pltpu.VMEM((count, depth, LANES), bf16),
            pltpu.VMEM((*grid, count * anchors, LANES), bf16),
            pltpu.VMEM((*grid, depth, width), bf16),
            pltpu.VMEM((*grid, depth, width), bf16),
            pltpu.SemaphoreType.DMA((6,)),
            pltpu.SemaphoreType.DMA((copies,)),
            pltpu.SemaphoreType.DMA((lines + PLANE,)),
            pltpu.SemaphoreType.DMA((count,)),
            pltpu.SemaphoreType.DMA((lines + PLANE,)),
            pltpu.SemaphoreType.DMA(grid),
            pltpu.SemaphoreType.DMA(grid),
            pltpu.SemaphoreType.DMA(grid),
            pltpu.SemaphoreType.DMA(grid),
        ],
        compiler_params=pltpu.CompilerParams(
            collective_id=0, has_side_effects=True, vmem_limit_bytes=60 * 1024 * 1024
        ),
        cost_estimate=pl.CostEstimate(
            flops=4 * padded * width * width, bytes_accessed=4 * width * width, transcendentals=0
        ),
    )(anchor_index, cells, queries, norm_gain.reshape(1, -1), w_qkv, w_out)


def solution(mesh):
    count, parts = mesh.shape["seq"], mesh.shape["geo"]

    def local(cells, anchor_index, queries, norm_gain, w_qkv, w_out):
        width = cells.shape[1]
        args = (cells, anchor_index, queries, norm_gain, w_qkv, w_out)
        tiles = (
            parts == 2
            and count % PLANE == 0
            and count * LANES == 2 * width
            and HEADS * LANES == 2 * width
            and count * anchor_index.shape[0] == LANES
        )
        if tiles:
            return fused(count // PLANE, *args)
        return gathered(*args)

    placed = (
        P(("geo", "seq"), None),
        P(("geo", "seq")),
        P(("geo", "seq"), None),
        P(),
        P("seq", None),
        P("seq", None),
    )
    return jax.shard_map(
        local,
        mesh=mesh,
        in_specs=placed,
        out_specs=(P(("geo", "seq"), None), P(("geo", "seq"), None)),
        check_vma=False,
    )
```

```python
import functools

import jax
import jax.numpy as jnp
from jax import lax
from jax.experimental import pallas as pl
from jax.experimental.pallas import tpu as pltpu
from jax.sharding import PartitionSpec as P

HEADS = 16
PLANE = 4
LANES = 128
MESH = pl.DeviceIdType.MESH


def normalize(rows, norm_gain):
    values = rows.astype(jnp.float32)
    scale = lax.rsqrt(jnp.mean(values * values, axis=-1, keepdims=True) + 1e-05)
    return (values * scale * norm_gain).astype(jnp.bfloat16)


def split_heads(rows, heads):
    return rows.reshape(rows.shape[0], heads, rows.shape[1] // heads).transpose(1, 0, 2)


def attend_whole(query_rows, key_rows, value_rows, heads):
    count, width = query_rows.shape
    factor = (width // heads) ** (-0.5)

    def single(items):
        qpart, kpart, vpart = items
        scores = jnp.dot(qpart, kpart.T, preferred_element_type=jnp.float32) * factor
        peak = jnp.max(scores, axis=-1, keepdims=True)
        expo = jnp.exp(scores - peak)
        total = jnp.sum(expo, axis=-1, keepdims=True)
        mixed = jnp.dot(expo.astype(jnp.bfloat16), vpart, preferred_element_type=jnp.float32)
        return (mixed / total).astype(jnp.bfloat16)

    result = lax.map(
        single,
        (
            split_heads(query_rows, heads),
            split_heads(key_rows, heads),
            split_heads(value_rows, heads),
        ),
    )
    return result.transpose(1, 0, 2).reshape(count, width)


def gathered(cells, anchor_index, queries, norm_gain, w_qkv, w_out):
    heads = HEADS
    width = cells.shape[1]
    anchor_rows = anchor_index.shape[0]
    local_index = anchor_index - lax.axis_index("seq") * cells.shape[0]
    anchors = jnp.take(cells, local_index, axis=0)
    norm_a = normalize(anchors, norm_gain)
    norm_q = normalize(queries, norm_gain)
    piece = lax.all_gather(w_qkv, "seq", axis=0, tiled=True)
    total_a = jnp.dot(norm_a, piece, preferred_element_type=jnp.float32)
    total_q = jnp.dot(norm_q, piece[:, :width], preferred_element_type=jnp.float32)
    qkv_a = total_a.astype(jnp.bfloat16)
    q_q = total_q.astype(jnp.bfloat16)
    all_query = jnp.concatenate([qkv_a[:, :width], q_q], axis=0)
    keys_values = lax.all_gather(qkv_a[:, width:], "seq", axis=0, tiled=True)
    context = attend_whole(all_query, keys_values[:, :width], keys_values[:, width:], heads)
    projected = jnp.dot(
        context,
        lax.all_gather(w_out, "seq", axis=0, tiled=True),
        preferred_element_type=jnp.float32,
    )
    projected = projected.astype(jnp.bfloat16)
    return (projected[:anchor_rows], projected[anchor_rows:])


def kernel(
    lines,
    index_ref,
    cells_hbm,
    queries_hbm,
    gain_hbm,
    w_qkv_ref,
    w_out_ref,
    anchor_out_ref,
    query_out_ref,
    cells_ref,
    queries_ref,
    gain_ref,
    norm_ref,
    q_ref,
    ctx_ref,
    na_all,
    wkv,
    kv_all,
    wq_all,
    wo_all,
    load_sem,
    send_sem,
    na_sem,
    a2a_sem,
    kv_sem,
    wq_sem,
    wo_sem,
    wq_sib_sem,
    wo_sib_sem,
):
    count = lines * PLANE
    me = lax.axis_index("seq")
    core = lax.axis_index("geo")
    line = me // PLANE
    spot = me % PLANE
    width = cells_ref.shape[1]
    half = width // 2
    mine = pl.ds(pl.multiple_of(core * half, LANES), half)
    other = pl.ds(pl.multiple_of((1 - core) * half, LANES), half)
    anchors = index_ref.shape[0]
    rows = queries_ref.shape[0]

    flip_x = 1 - 2 * (spot % 2)
    flip_y = 2 - 4 * (spot // 2)
    near = spot + flip_x * (1 - core) + flip_y * core
    far = spot + flip_y * (1 - core) + flip_x * core
    cross = spot + flip_x + flip_y

    barrier = pltpu.get_barrier_semaphore()
    for k in range(1, count):
        pl.semaphore_signal(
            barrier, inc=1, device_id={"seq": (me + k) % count}, device_id_type=MESH
        )
    pl.semaphore_signal(barrier, inc=1, device_id={"geo": 1 - core}, device_id_type=MESH)

    start = pl.multiple_of(width + me * LANES, LANES)
    share = w_qkv_ref.shape[0] // 2
    part = pl.ds(pl.multiple_of(core * share, share), share)
    rest = pl.ds(pl.multiple_of((1 - core) * share, share), share)
    loads = []
    for source, target in (
        (cells_hbm, cells_ref),
        (gain_hbm, gain_ref),
        (w_qkv_ref.at[:, pl.ds(0, width)], wq_all.at[line, spot]),
        (w_qkv_ref.at[part, pl.ds(start, LANES)], wkv.at[me, part]),
        (w_out_ref, wo_all.at[line, spot]),
        (queries_hbm, queries_ref),
    ):
        load = pltpu.make_async_copy(source, target, load_sem.at[len(loads)])
        load.start()
        loads.append(load)

    started = []

    def send(src, dst, sem, target):
        copy = pltpu.make_async_remote_copy(
            src_ref=src,
            dst_ref=dst,
            send_sem=send_sem.at[len(started)],
            recv_sem=sem,
            device_id=target,
            device_id_type=MESH,
        )
        copy.start()
        started.append(copy)

    def arrived(dst, sem):
        pltpu.make_async_remote_copy(
            src_ref=dst,
            dst_ref=dst,
            send_sem=send_sem.at[0],
            recv_sem=sem,
            device_id={"geo": 1 - core},
            device_id_type=MESH,
        ).wait_recv()

    loads[0].wait()
    loads[1].wait()
    gain = gain_ref[...]

    row = lax.broadcasted_iota(jnp.int32, (anchors, cells_ref.shape[0]), 0)
    column = lax.broadcasted_iota(jnp.int32, (anchors, cells_ref.shape[0]), 1)
    wanted = jnp.zeros_like(row)
    for a in range(anchors):
        wanted = jnp.where(row == a, index_ref[a] - me * cells_ref.shape[0], wanted)
    pick = jnp.where(wanted == column, 1.0, 0.0).astype(jnp.bfloat16)
    picked = jnp.dot(pick, cells_ref[...], preferred_element_type=jnp.float32)
    scale = lax.rsqrt(jnp.mean(picked * picked, axis=-1, keepdims=True) + 1e-05)
    norm_a = picked * scale * gain
    na_all[line, spot] = jnp.concatenate([norm_a[:, :half], norm_a[:, half:]], axis=0).astype(
        jnp.bfloat16
    )
    norm_ref[pl.ds(rows, 2 * anchors), :] = jnp.concatenate([norm_a, norm_a], axis=0).astype(
        jnp.bfloat16
    )
    for load in loads[2:5]:
        load.wait()

    pl.semaphore_wait(barrier, count)

    def on_line(k):
        return (line + k) % lines

    def on_plane(k):
        return (spot + k) % PLANE

    def line_target(k):
        return {"seq": on_line(k) * PLANE + spot}

    def plane_target(where):
        return {"seq": line * PLANE + where}

    sibling = {"geo": 1 - core}

    def to_line(whole, sem):
        block = whole.at[line, spot, :, mine]
        for k in range(1, lines):
            send(block, block, sem.at[line, spot], line_target(k))

    def to_plane(whole, sem, at):
        block = whole.at[at, spot, :, mine]
        send(block, block, sem.at[at, spot], plane_target(near))
        send(block, block, sem.at[at, spot], plane_target(far))

    def to_cross(whole, sem, at):
        block = whole.at[at, near, :, mine]
        send(block, block, sem.at[at, near], plane_target(far))

    def to_sibling(whole, sem, at, where):
        block = whole.at[at, where, :, mine]
        send(block, block, sem.at[at, where], sibling)

    def weight_arrived(whole, sem, at, where):
        arrived(whole.at[at, where, :, mine], sem.at[at, where])

    for k in range(1, lines):
        block = na_all.at[line, spot]
        send(block, block, na_sem.at[line], line_target(k))
    for k in range(1, count):
        to = (me + k) % count
        start = pl.multiple_of(width + to * LANES, LANES)
        block = w_qkv_ref.at[part, pl.ds(start, LANES)]
        send(block, wkv.at[me, part], a2a_sem.at[me], {"seq": to})

    for k in range(1, lines):
        arrived(na_all.at[on_line(k), spot], na_sem.at[on_line(k)])
    for k in range(1, PLANE):
        block = na_all.at[:, spot]
        send(block, block, na_sem.at[lines + spot], plane_target(on_plane(k)))
    to_line(wq_all, wq_sem)
    to_plane(wq_all, wq_sem, line)

    loads[5].wait()
    values = queries_ref[...].astype(jnp.float32)
    scale = lax.rsqrt(jnp.mean(values * values, axis=-1, keepdims=True) + 1e-05)
    norm_ref[pl.ds(0, rows), :] = (values * scale * gain).astype(jnp.bfloat16)

    for k in range(1, count):
        source = (me + k) % count
        arrived(wkv.at[source, part], a2a_sem.at[source])
    send(wkv.at[:, part], wkv.at[:, part], a2a_sem.at[count], sibling)
    for k in range(1, PLANE):
        arrived(na_all.at[:, on_plane(k)], na_sem.at[lines + on_plane(k)])
    arrived(wkv.at[:, rest], a2a_sem.at[count])
    packed = na_all[...].reshape(count * 2 * anchors, half)
    slab = wkv[...].reshape(width, LANES)
    low = jnp.dot(packed, slab[:half], preferred_element_type=jnp.float32)
    high = jnp.dot(packed, slab[half:], preferred_element_type=jnp.float32)
    low = low.reshape(count, 2 * anchors, LANES)[:, :anchors]
    high = high.reshape(count, 2 * anchors, LANES)[:, anchors:]
    kv_all[line, spot] = (low + high).reshape(count * anchors, LANES).astype(jnp.bfloat16)

    for k in range(1, lines):
        block = kv_all.at[line, spot]
        send(block, block, kv_sem.at[line], line_target(k))
    for k in range(1, lines):
        at = on_line(k)
        weight_arrived(wq_all, wq_sem, at, spot)
        to_plane(wq_all, wq_sem, at)
        to_sibling(wq_all, wq_sib_sem, at, spot)
    to_line(wo_all, wo_sem)
    for k in range(lines):
        weight_arrived(wq_all, wq_sem, on_line(k), near)
        to_cross(wq_all, wq_sem, on_line(k))
        to_sibling(wq_all, wq_sib_sem, on_line(k), near)
    for k in range(1, lines):
        arrived(kv_all.at[on_line(k), spot], kv_sem.at[on_line(k)])
    block = kv_all.at[:, spot]
    send(block, block, kv_sem.at[lines + spot], plane_target(near))
    send(block, block, kv_sem.at[lines + spot], plane_target(far))
    to_plane(wo_all, wo_sem, line)
    for k in range(1, lines):
        at = on_line(k)
        weight_arrived(wo_all, wo_sem, at, spot)
        to_plane(wo_all, wo_sem, at)
        to_sibling(wo_all, wo_sib_sem, at, spot)
    arrived(kv_all.at[:, near], kv_sem.at[lines + near])
    block = kv_all.at[:, near]
    send(block, block, kv_sem.at[lines + near], plane_target(far))

    for where in (far, cross):
        for k in range(lines):
            weight_arrived(wq_all, wq_sem, on_line(k), where)
            to_sibling(wq_all, wq_sib_sem, on_line(k), where)

    def from_sibling(whole, sib_sem):
        for j in range(lines):
            for k in range(PLANE):
                if j or k:
                    at, where = on_line(j), on_plane(k)
                    arrived(whole.at[at, where, :, other], sib_sem.at[at, where])

    from_sibling(wq_all, wq_sib_sem)
    step = 2 * LANES

    later = [(on_line(k), near) for k in range(lines)]
    later += [(on_line(k), far) for k in range(lines)]
    later += [(on_line(k), cross) for k in range(lines)]

    def pass_on(steps):
        for _ in range(steps):
            if later:
                first = len(later) > 2 * lines
                at, where = later.pop(0)
                weight_arrived(wo_all, wo_sem, at, where)
                if first:
                    to_cross(wo_all, wo_sem, at)
                to_sibling(wo_all, wo_sib_sem, at, where)

    for j in range(width // step):
        columns = pl.ds(j * step, step)
        block = wq_all[:, :, :, columns].reshape(width, step)
        q_ref[:, columns] = jnp.dot(
            norm_ref[...], block, preferred_element_type=jnp.float32
        ).astype(jnp.bfloat16)

    arrived(kv_all.at[:, far], kv_sem.at[lines + far])
    arrived(kv_all.at[:, cross], kv_sem.at[lines + cross])

    head = width // HEADS
    factor = head ** (-0.5)
    keys = count * anchors
    upper = lax.broadcasted_iota(jnp.int32, (keys, LANES), 1) >= head
    upper_ctx = lax.broadcasted_iota(jnp.int32, (norm_ref.shape[0], LANES), 1) >= head

    def blocks(pair):
        block = kv_all[pair // PLANE, pair % PLANE]
        zero = jnp.zeros_like(block)
        return jnp.concatenate([jnp.where(upper, zero, block), jnp.where(upper, block, zero)], axis=0)

    pairs = HEADS // 2
    for pair in range(pairs):
        pass_on(2)
        columns = pl.ds(pair * LANES, LANES)
        scores = lax.dot_general(
            q_ref[:, columns],
            blocks(pair),
            (((1,), (1,)), ((), ())),
            preferred_element_type=jnp.float32,
        )
        scores = scores * factor
        expos, totals = [], []
        for side in range(2):
            part = scores[:, side * keys : (side + 1) * keys]
            expo = jnp.exp(part - jnp.max(part, axis=-1, keepdims=True))
            totals.append(jnp.sum(expo, axis=-1, keepdims=True))
            expos.append(expo.astype(jnp.bfloat16))
        mixed = jnp.dot(
            jnp.concatenate(expos, axis=1), blocks(pairs + pair), preferred_element_type=jnp.float32
        )
        total = jnp.where(upper_ctx, totals[1], totals[0])
        ctx_ref[:, columns] = (mixed / total).astype(jnp.bfloat16)

    pass_on(len(later))
    from_sibling(wo_all, wo_sib_sem)
    for j in range(width // step):
        columns = pl.ds(j * step, step)
        block = wo_all[:, :, :, columns].reshape(width, step)
        result = jnp.dot(ctx_ref[...], block, preferred_element_type=jnp.float32)
        query_out_ref[:, columns] = result[:rows].astype(jnp.bfloat16)
        anchor_out_ref[:, columns] = result[rows : rows + anchors].astype(jnp.bfloat16)

    for copy in started:
        copy.wait_send()


def fused(lines, cells, anchor_index, queries, norm_gain, w_qkv, w_out):
    rows, width = queries.shape
    anchors = anchor_index.shape[0]
    depth = w_out.shape[0]
    count = lines * PLANE
    padded = rows + 2 * anchors
    vmem = pl.BlockSpec(memory_space=pltpu.VMEM)
    grid = (lines, PLANE)
    bf16 = jnp.bfloat16
    copies = 2 * (lines - 1 + PLANE - 1) + count
    copies += 2 * (lines - 1 + lines * (PLANE - 1) + count - 1)
    hbm = pl.BlockSpec(memory_space=pltpu.HBM)
    return pl.pallas_call(
        functools.partial(kernel, lines),
        out_shape=(
            jax.ShapeDtypeStruct((anchors, width), bf16),
            jax.ShapeDtypeStruct((rows, width), bf16),
        ),
        in_specs=[pl.BlockSpec(memory_space=pltpu.SMEM)] + [hbm] * 5,
        out_specs=(vmem, vmem),
        scratch_shapes=[
            pltpu.VMEM(cells.shape, bf16),
            pltpu.VMEM(queries.shape, bf16),
            pltpu.VMEM((1, width), jnp.float32),
            pltpu.VMEM((padded, width), bf16),
            pltpu.VMEM((padded, width), bf16),
            pltpu.VMEM((padded, width), bf16),
            pltpu.VMEM((*grid, 2 * anchors, width // 2), bf16),
            pltpu.VMEM((count, depth, LANES), bf16),
            pltpu.VMEM((*grid, count * anchors, LANES), bf16),
            pltpu.VMEM((*grid, depth, width), bf16),
            pltpu.VMEM((*grid, depth, width), bf16),
            pltpu.SemaphoreType.DMA((6,)),
            pltpu.SemaphoreType.DMA((copies,)),
            pltpu.SemaphoreType.DMA((lines + PLANE,)),
            pltpu.SemaphoreType.DMA((count + 1,)),
            pltpu.SemaphoreType.DMA((lines + PLANE,)),
            pltpu.SemaphoreType.DMA(grid),
            pltpu.SemaphoreType.DMA(grid),
            pltpu.SemaphoreType.DMA(grid),
            pltpu.SemaphoreType.DMA(grid),
        ],
        compiler_params=pltpu.CompilerParams(
            collective_id=0, has_side_effects=True, vmem_limit_bytes=60 * 1024 * 1024
        ),
        cost_estimate=pl.CostEstimate(
            flops=4 * padded * width * width, bytes_accessed=4 * width * width, transcendentals=0
        ),
    )(anchor_index, cells, queries, norm_gain.reshape(1, -1), w_qkv, w_out)


def solution(mesh):
    count, parts = mesh.shape["seq"], mesh.shape["geo"]

    def local(cells, anchor_index, queries, norm_gain, w_qkv, w_out):
        width = cells.shape[1]
        args = (cells, anchor_index, queries, norm_gain, w_qkv, w_out)
        tiles = (
            parts == 2
            and count % PLANE == 0
            and count * LANES == 2 * width
            and HEADS * LANES == 2 * width
            and count * anchor_index.shape[0] == LANES
            and w_qkv.shape[0] % 32 == 0
        )
        if tiles:
            return fused(count // PLANE, *args)
        return gathered(*args)

    placed = (
        P(("geo", "seq"), None),
        P(("geo", "seq")),
        P(("geo", "seq"), None),
        P(),
        P("seq", None),
        P("seq", None),
    )
    return jax.shard_map(
        local,
        mesh=mesh,
        in_specs=placed,
        out_specs=(P(("geo", "seq"), None), P(("geo", "seq"), None)),
        check_vma=False,
    )
```

```python
import functools

import jax
import jax.numpy as jnp
from jax import lax
from jax.experimental import pallas as pl
from jax.experimental.pallas import tpu as pltpu
from jax.sharding import PartitionSpec as P

HEADS = 16
PLANE = 4
LANES = 128
MESH = pl.DeviceIdType.MESH


def normalize(rows, norm_gain):
    values = rows.astype(jnp.float32)
    scale = lax.rsqrt(jnp.mean(values * values, axis=-1, keepdims=True) + 1e-05)
    return (values * scale * norm_gain).astype(jnp.bfloat16)


def split_heads(rows, heads):
    return rows.reshape(rows.shape[0], heads, rows.shape[1] // heads).transpose(1, 0, 2)


def attend_whole(query_rows, key_rows, value_rows, heads):
    count, width = query_rows.shape
    factor = (width // heads) ** (-0.5)

    def single(items):
        qpart, kpart, vpart = items
        scores = jnp.dot(qpart, kpart.T, preferred_element_type=jnp.float32) * factor
        peak = jnp.max(scores, axis=-1, keepdims=True)
        expo = jnp.exp(scores - peak)
        total = jnp.sum(expo, axis=-1, keepdims=True)
        mixed = jnp.dot(expo.astype(jnp.bfloat16), vpart, preferred_element_type=jnp.float32)
        return (mixed / total).astype(jnp.bfloat16)

    result = lax.map(
        single,
        (
            split_heads(query_rows, heads),
            split_heads(key_rows, heads),
            split_heads(value_rows, heads),
        ),
    )
    return result.transpose(1, 0, 2).reshape(count, width)


def gathered(cells, anchor_index, queries, norm_gain, w_qkv, w_out):
    heads = HEADS
    width = cells.shape[1]
    anchor_rows = anchor_index.shape[0]
    local_index = anchor_index - lax.axis_index("seq") * cells.shape[0]
    anchors = jnp.take(cells, local_index, axis=0)
    norm_a = normalize(anchors, norm_gain)
    norm_q = normalize(queries, norm_gain)
    piece = lax.all_gather(w_qkv, "seq", axis=0, tiled=True)
    total_a = jnp.dot(norm_a, piece, preferred_element_type=jnp.float32)
    total_q = jnp.dot(norm_q, piece[:, :width], preferred_element_type=jnp.float32)
    qkv_a = total_a.astype(jnp.bfloat16)
    q_q = total_q.astype(jnp.bfloat16)
    all_query = jnp.concatenate([qkv_a[:, :width], q_q], axis=0)
    keys_values = lax.all_gather(qkv_a[:, width:], "seq", axis=0, tiled=True)
    context = attend_whole(all_query, keys_values[:, :width], keys_values[:, width:], heads)
    projected = jnp.dot(
        context,
        lax.all_gather(w_out, "seq", axis=0, tiled=True),
        preferred_element_type=jnp.float32,
    )
    projected = projected.astype(jnp.bfloat16)
    return (projected[:anchor_rows], projected[anchor_rows:])


def kernel(
    lines,
    index_ref,
    cells_hbm,
    queries_hbm,
    gain_hbm,
    w_qkv_ref,
    w_out_ref,
    anchor_out_ref,
    query_out_ref,
    cells_ref,
    queries_ref,
    gain_ref,
    norm_ref,
    q_ref,
    ctx_ref,
    na_all,
    wkv,
    kv_all,
    wq_all,
    wo_all,
    load_sem,
    send_sem,
    na_sem,
    a2a_sem,
    kv_sem,
    wq_sem,
    wo_sem,
    wq_sib_sem,
    wo_sib_sem,
):
    count = lines * PLANE
    me = lax.axis_index("seq")
    core = lax.axis_index("geo")
    line = me // PLANE
    spot = me % PLANE
    width = cells_ref.shape[1]
    half = width // 2
    mine = pl.ds(pl.multiple_of(core * half, LANES), half)
    other = pl.ds(pl.multiple_of((1 - core) * half, LANES), half)
    anchors = index_ref.shape[0]
    rows = queries_ref.shape[0]

    flip_x = 1 - 2 * (spot % 2)
    flip_y = 2 - 4 * (spot // 2)
    near = spot + flip_x * (1 - core) + flip_y * core
    far = spot + flip_y * (1 - core) + flip_x * core
    cross = spot + flip_x + flip_y

    barrier = pltpu.get_barrier_semaphore()
    for k in range(1, count):
        pl.semaphore_signal(
            barrier, inc=1, device_id={"seq": (me + k) % count}, device_id_type=MESH
        )
    pl.semaphore_signal(barrier, inc=1, device_id={"geo": 1 - core}, device_id_type=MESH)

    start = pl.multiple_of(width + me * LANES, LANES)
    share = w_qkv_ref.shape[0] // 2
    part = pl.ds(pl.multiple_of(core * share, share), share)
    rest = pl.ds(pl.multiple_of((1 - core) * share, share), share)
    loads = []
    for source, target in (
        (cells_hbm, cells_ref),
        (gain_hbm, gain_ref),
        (w_qkv_ref.at[:, pl.ds(0, width)], wq_all.at[line, spot]),
        (w_qkv_ref.at[part, pl.ds(start, LANES)], wkv.at[me, part]),
        (w_out_ref, wo_all.at[line, spot]),
        (queries_hbm, queries_ref),
    ):
        load = pltpu.make_async_copy(source, target, load_sem.at[len(loads)])
        load.start()
        loads.append(load)

    started = []

    def send(src, dst, sem, target):
        copy = pltpu.make_async_remote_copy(
            src_ref=src,
            dst_ref=dst,
            send_sem=send_sem.at[len(started)],
            recv_sem=sem,
            device_id=target,
            device_id_type=MESH,
        )
        copy.start()
        started.append(copy)

    def arrived(dst, sem):
        pltpu.make_async_remote_copy(
            src_ref=dst,
            dst_ref=dst,
            send_sem=send_sem.at[0],
            recv_sem=sem,
            device_id={"geo": 1 - core},
            device_id_type=MESH,
        ).wait_recv()

    loads[0].wait()
    loads[1].wait()
    gain = gain_ref[...]

    row = lax.broadcasted_iota(jnp.int32, (anchors, cells_ref.shape[0]), 0)
    column = lax.broadcasted_iota(jnp.int32, (anchors, cells_ref.shape[0]), 1)
    wanted = jnp.zeros_like(row)
    for a in range(anchors):
        wanted = jnp.where(row == a, index_ref[a] - me * cells_ref.shape[0], wanted)
    pick = jnp.where(wanted == column, 1.0, 0.0).astype(jnp.bfloat16)
    picked = jnp.dot(pick, cells_ref[...], preferred_element_type=jnp.float32)
    scale = lax.rsqrt(jnp.mean(picked * picked, axis=-1, keepdims=True) + 1e-05)
    norm_a = picked * scale * gain
    na_all[line, spot] = jnp.concatenate([norm_a[:, :half], norm_a[:, half:]], axis=0).astype(
        jnp.bfloat16
    )
    norm_ref[pl.ds(rows, 2 * anchors), :] = jnp.concatenate([norm_a, norm_a], axis=0).astype(
        jnp.bfloat16
    )
    for load in loads[2:5]:
        load.wait()

    pl.semaphore_wait(barrier, count)

    def on_line(k):
        return (line + k) % lines

    def on_plane(k):
        return (spot + k) % PLANE

    def line_target(k):
        return {"seq": on_line(k) * PLANE + spot}

    def plane_target(where):
        return {"seq": line * PLANE + where}

    sibling = {"geo": 1 - core}

    def to_line(whole, sem):
        block = whole.at[line, spot, :, mine]
        for k in range(1, lines):
            send(block, block, sem.at[line, spot], line_target(k))

    def to_plane(whole, sem, at):
        block = whole.at[at, spot, :, mine]
        send(block, block, sem.at[at, spot], plane_target(near))
        send(block, block, sem.at[at, spot], plane_target(far))

    def to_cross(whole, sem, at):
        block = whole.at[at, near, :, mine]
        send(block, block, sem.at[at, near], plane_target(far))

    def to_sibling(whole, sem, at, where):
        block = whole.at[at, where, :, mine]
        send(block, block, sem.at[at, where], sibling)

    def weight_arrived(whole, sem, at, where):
        arrived(whole.at[at, where, :, mine], sem.at[at, where])

    for k in range(1, lines):
        block = na_all.at[line, spot]
        send(block, block, na_sem.at[line], line_target(k))
    for k in range(1, count):
        to = (me + k) % count
        start = pl.multiple_of(width + to * LANES, LANES)
        block = w_qkv_ref.at[part, pl.ds(start, LANES)]
        send(block, wkv.at[me, part], a2a_sem.at[me], {"seq": to})

    for k in range(1, lines):
        arrived(na_all.at[on_line(k), spot], na_sem.at[on_line(k)])
    for k in range(1, PLANE):
        block = na_all.at[:, spot]
        send(block, block, na_sem.at[lines + spot], plane_target(on_plane(k)))
    to_line(wq_all, wq_sem)
    to_plane(wq_all, wq_sem, line)

    loads[5].wait()
    values = queries_ref[...].astype(jnp.float32)
    scale = lax.rsqrt(jnp.mean(values * values, axis=-1, keepdims=True) + 1e-05)
    norm_ref[pl.ds(0, rows), :] = (values * scale * gain).astype(jnp.bfloat16)

    for k in range(1, count):
        source = (me + k) % count
        arrived(wkv.at[source, part], a2a_sem.at[source])
    send(wkv.at[:, part], wkv.at[:, part], a2a_sem.at[count], sibling)
    for k in range(1, lines):
        at = on_line(k)
        weight_arrived(wq_all, wq_sem, at, spot)
        to_plane(wq_all, wq_sem, at)
        to_sibling(wq_all, wq_sib_sem, at, spot)
    for k in range(1, PLANE):
        arrived(na_all.at[:, on_plane(k)], na_sem.at[lines + on_plane(k)])
    arrived(wkv.at[:, rest], a2a_sem.at[count])
    packed = na_all[...].reshape(count * 2 * anchors, half)
    slab = wkv[...].reshape(width, LANES)
    low = jnp.dot(packed, slab[:half], preferred_element_type=jnp.float32)
    high = jnp.dot(packed, slab[half:], preferred_element_type=jnp.float32)
    low = low.reshape(count, 2 * anchors, LANES)[:, :anchors]
    high = high.reshape(count, 2 * anchors, LANES)[:, anchors:]
    kv_all[line, spot] = (low + high).reshape(count * anchors, LANES).astype(jnp.bfloat16)

    for k in range(1, lines):
        block = kv_all.at[line, spot]
        send(block, block, kv_sem.at[line], line_target(k))
    to_line(wo_all, wo_sem)
    for k in range(lines):
        weight_arrived(wq_all, wq_sem, on_line(k), near)
        to_cross(wq_all, wq_sem, on_line(k))
        to_sibling(wq_all, wq_sib_sem, on_line(k), near)
    for k in range(1, lines):
        arrived(kv_all.at[on_line(k), spot], kv_sem.at[on_line(k)])
    block = kv_all.at[:, spot]
    send(block, block, kv_sem.at[lines + spot], plane_target(near))
    send(block, block, kv_sem.at[lines + spot], plane_target(far))
    to_plane(wo_all, wo_sem, line)
    for k in range(1, lines):
        at = on_line(k)
        weight_arrived(wo_all, wo_sem, at, spot)
        to_plane(wo_all, wo_sem, at)
        to_sibling(wo_all, wo_sib_sem, at, spot)
    arrived(kv_all.at[:, near], kv_sem.at[lines + near])
    block = kv_all.at[:, near]
    send(block, block, kv_sem.at[lines + near], plane_target(far))

    for where in (far, cross):
        for k in range(lines):
            weight_arrived(wq_all, wq_sem, on_line(k), where)
            to_sibling(wq_all, wq_sib_sem, on_line(k), where)

    def from_sibling(whole, sib_sem):
        for j in range(lines):
            for k in range(PLANE):
                if j or k:
                    at, where = on_line(j), on_plane(k)
                    arrived(whole.at[at, where, :, other], sib_sem.at[at, where])

    from_sibling(wq_all, wq_sib_sem)
    step = 2 * LANES

    later = [(on_line(k), near) for k in range(lines)]
    later += [(on_line(k), far) for k in range(lines)]
    later += [(on_line(k), cross) for k in range(lines)]

    def pass_on(steps):
        for _ in range(steps):
            if later:
                first = len(later) > 2 * lines
                at, where = later.pop(0)
                weight_arrived(wo_all, wo_sem, at, where)
                if first:
                    to_cross(wo_all, wo_sem, at)
                to_sibling(wo_all, wo_sib_sem, at, where)

    for j in range(width // step):
        columns = pl.ds(j * step, step)
        block = wq_all[:, :, :, columns].reshape(width, step)
        q_ref[:, columns] = jnp.dot(
            norm_ref[...], block, preferred_element_type=jnp.float32
        ).astype(jnp.bfloat16)

    arrived(kv_all.at[:, far], kv_sem.at[lines + far])
    arrived(kv_all.at[:, cross], kv_sem.at[lines + cross])

    head = width // HEADS
    factor = head ** (-0.5)
    keys = count * anchors
    upper = lax.broadcasted_iota(jnp.int32, (keys, LANES), 1) >= head
    upper_ctx = lax.broadcasted_iota(jnp.int32, (norm_ref.shape[0], LANES), 1) >= head

    def blocks(pair):
        block = kv_all[pair // PLANE, pair % PLANE]
        zero = jnp.zeros_like(block)
        return jnp.concatenate([jnp.where(upper, zero, block), jnp.where(upper, block, zero)], axis=0)

    pairs = HEADS // 2
    for pair in range(pairs):
        pass_on(2)
        columns = pl.ds(pair * LANES, LANES)
        scores = lax.dot_general(
            q_ref[:, columns],
            blocks(pair),
            (((1,), (1,)), ((), ())),
            preferred_element_type=jnp.float32,
        )
        scores = scores * factor
        expos, totals = [], []
        for side in range(2):
            part = scores[:, side * keys : (side + 1) * keys]
            expo = jnp.exp(part - jnp.max(part, axis=-1, keepdims=True))
            totals.append(jnp.sum(expo, axis=-1, keepdims=True))
            expos.append(expo.astype(jnp.bfloat16))
        mixed = jnp.dot(
            jnp.concatenate(expos, axis=1), blocks(pairs + pair), preferred_element_type=jnp.float32
        )
        total = jnp.where(upper_ctx, totals[1], totals[0])
        ctx_ref[:, columns] = (mixed / total).astype(jnp.bfloat16)

    pass_on(len(later))
    from_sibling(wo_all, wo_sib_sem)
    for j in range(width // step):
        columns = pl.ds(j * step, step)
        block = wo_all[:, :, :, columns].reshape(width, step)
        result = jnp.dot(ctx_ref[...], block, preferred_element_type=jnp.float32)
        query_out_ref[:, columns] = result[:rows].astype(jnp.bfloat16)
        anchor_out_ref[:, columns] = result[rows : rows + anchors].astype(jnp.bfloat16)

    for copy in started:
        copy.wait_send()


def fused(lines, cells, anchor_index, queries, norm_gain, w_qkv, w_out):
    rows, width = queries.shape
    anchors = anchor_index.shape[0]
    depth = w_out.shape[0]
    count = lines * PLANE
    padded = rows + 2 * anchors
    vmem = pl.BlockSpec(memory_space=pltpu.VMEM)
    grid = (lines, PLANE)
    bf16 = jnp.bfloat16
    copies = 2 * (lines - 1 + PLANE - 1) + count
    copies += 2 * (lines - 1 + lines * (PLANE - 1) + count - 1)
    hbm = pl.BlockSpec(memory_space=pltpu.HBM)
    return pl.pallas_call(
        functools.partial(kernel, lines),
        out_shape=(
            jax.ShapeDtypeStruct((anchors, width), bf16),
            jax.ShapeDtypeStruct((rows, width), bf16),
        ),
        in_specs=[pl.BlockSpec(memory_space=pltpu.SMEM)] + [hbm] * 5,
        out_specs=(vmem, vmem),
        scratch_shapes=[
            pltpu.VMEM(cells.shape, bf16),
            pltpu.VMEM(queries.shape, bf16),
            pltpu.VMEM((1, width), jnp.float32),
            pltpu.VMEM((padded, width), bf16),
            pltpu.VMEM((padded, width), bf16),
            pltpu.VMEM((padded, width), bf16),
            pltpu.VMEM((*grid, 2 * anchors, width // 2), bf16),
            pltpu.VMEM((count, depth, LANES), bf16),
            pltpu.VMEM((*grid, count * anchors, LANES), bf16),
            pltpu.VMEM((*grid, depth, width), bf16),
            pltpu.VMEM((*grid, depth, width), bf16),
            pltpu.SemaphoreType.DMA((6,)),
            pltpu.SemaphoreType.DMA((copies,)),
            pltpu.SemaphoreType.DMA((lines + PLANE,)),
            pltpu.SemaphoreType.DMA((count + 1,)),
            pltpu.SemaphoreType.DMA((lines + PLANE,)),
            pltpu.SemaphoreType.DMA(grid),
            pltpu.SemaphoreType.DMA(grid),
            pltpu.SemaphoreType.DMA(grid),
            pltpu.SemaphoreType.DMA(grid),
        ],
        compiler_params=pltpu.CompilerParams(
            collective_id=0, has_side_effects=True, vmem_limit_bytes=60 * 1024 * 1024
        ),
        cost_estimate=pl.CostEstimate(
            flops=4 * padded * width * width, bytes_accessed=4 * width * width, transcendentals=0
        ),
    )(anchor_index, cells, queries, norm_gain.reshape(1, -1), w_qkv, w_out)


def solution(mesh):
    count, parts = mesh.shape["seq"], mesh.shape["geo"]

    def local(cells, anchor_index, queries, norm_gain, w_qkv, w_out):
        width = cells.shape[1]
        args = (cells, anchor_index, queries, norm_gain, w_qkv, w_out)
        tiles = (
            parts == 2
            and count % PLANE == 0
            and count * LANES == 2 * width
            and HEADS * LANES == 2 * width
            and count * anchor_index.shape[0] == LANES
            and w_qkv.shape[0] % 32 == 0
        )
        if tiles:
            return fused(count // PLANE, *args)
        return gathered(*args)

    placed = (
        P(("geo", "seq"), None),
        P(("geo", "seq")),
        P(("geo", "seq"), None),
        P(),
        P("seq", None),
        P("seq", None),
    )
    return jax.shard_map(
        local,
        mesh=mesh,
        in_specs=placed,
        out_specs=(P(("geo", "seq"), None), P(("geo", "seq"), None)),
        check_vma=False,
    )
```
